256 devices in a mesh: outer: 16 (over z, core), inner: 16 (over x, y).
Axes of the slice: x: 4, y: 4, z: 8, core: 2. Of those that a mesh axis runs over, the one named last changes fastest.
Arguments:
- leaf_blocks: float32 [256, 512, 512], P(('outer', 'inner')), as said below
- leaf_bases: float32 [256, 512, 256], P(('outer', 'inner'))
- local_gens: float32 [256, 2, 256, 256], P(('outer', 'inner'))
- chain_gens: float32 [1024, 2, 256, 256], P(('outer', 'inner')), as said below
- node_ranks: int32 [5, 256], replicated, may hold values from 192 to 256, as said below
Outputs:
- local_reduced: float32 [256, 256, 256], P(('outer', 'inner'))
- chain_reduced: float32 [1024, 256, 256], P(('outer', 'inner'))
- top_factor: float32 [131072, 512], P(('outer', 'inner'))
The draws below stay inside these ranges and needn't reach their ends.
Inputs may be any that keep to these rules, and one draw needn't show every extreme that they name: `node_ranks`: ranks of all tree levels, entry [v, k] read for k < 256 >> v; both ends of the range occur in every draw. `leaf_blocks`: each leaf block is symmetric positive definite. Rows of chain_gens that belong to the same node are equal on all devices below that node.
All inputs are finite; a program needn't handle non-finite values.
Results may differ from the reference program's by a relative error of at most 0.00017.
Values sent between devices are 32-bit elements; how exact they have to be, the bound alone decides.
No kernel may reach another device: no remote copies, remote signals or barrier semaphores. Data moves between devices by JAX's collectives and lax.ppermute only.
A program may use at most 128 MiB of HBM per device.

```python
import math
import jax
import jax.numpy as jnp
from jax import lax

RANK = 256
LEAF = 512
LEAF_DEV = 1
LOCAL_LEVELS = 0
IN_LEVELS = 4
LEVELS = 5
LOCAL_NODES = 1
LEAVES = 256
DEVICES = 256


def random_noise(key, shape):
    return jax.random.normal(key, shape, jnp.float32)


def node_gens(key, level_id, node_id):
    node_key = jax.random.fold_in(jax.random.fold_in(key, level_id + 101), node_id)
    key_transfer, key_diagonal, key_coupling = jax.random.split(node_key, 3)
    row_ids = jnp.arange(RANK, dtype=jnp.int32)[:, None]
    col_ids = jnp.arange(RANK, dtype=jnp.int32)[None, :]
    is_odd = node_id % 2 == 1
    target = jnp.where(is_odd, 2 * col_ids - RANK, 2 * col_ids)
    in_half = jnp.where(is_odd, col_ids >= RANK // 2, col_ids < RANK // 2)
    dominant = ((row_ids == target) & in_half).astype(jnp.float32)
    transfer = dominant + random_noise(key_transfer, (RANK, RANK)) * (0.25 / math.sqrt(2 * RANK))
    diagonal = jax.random.uniform(key_diagonal, (RANK,), jnp.float32, -0.25, 0.25)
    coupling = jnp.diag(diagonal) + random_noise(key_coupling, (RANK, RANK)) * (0.06 / math.sqrt(RANK))
    return jnp.stack([transfer, coupling])


def draw_leaf_blocks(key, part):
    key_diagonal, key_noise = jax.random.split(jax.random.fold_in(key, 11))
    diagonal = jnp.exp(jax.random.uniform(key_diagonal, (LEAVES, LEAF), jnp.float32, math.log(3.0), math.log(8.0)))
    random_part = random_noise(key_noise, (LEAVES, LEAF, LEAF))
    symmetric = (random_part + jnp.swapaxes(random_part, 1, 2)) * (1.0 / math.sqrt(2.0 * LEAF))
    return symmetric + diagonal[:, :, None] * jnp.eye(LEAF, dtype=jnp.float32)[None, :, :]


def draw_leaf_bases(key, part):
    key_noise = jax.random.fold_in(key, 12)
    row_ids = jnp.arange(LEAF, dtype=jnp.int32)[:, None]
    col_ids = jnp.arange(RANK, dtype=jnp.int32)[None, :]
    dominant = (row_ids == 2 * col_ids).astype(jnp.float32)
    return dominant[None, :, :] + random_noise(key_noise, (LEAVES, LEAF, RANK)) * (0.25 / math.sqrt(LEAF))


def draw_local_gens(key, part):
    levels, positions, counts = ([], [], [])
    for tree_level in range(LOCAL_LEVELS + 1):
        per_device = LEAF_DEV >> tree_level
        for position in range(per_device):
            levels.append(tree_level)
            positions.append(position)
            counts.append(per_device)
    device = jnp.arange(DEVICES, dtype=jnp.int32)[:, None]
    level_ids = jnp.broadcast_to(jnp.array(levels, jnp.int32)[None, :], (DEVICES, LOCAL_NODES))
    node_ids = device * jnp.array(counts, jnp.int32)[None, :] + jnp.array(positions, jnp.int32)[None, :]
    gen_key = jax.random.fold_in(key, 13)
    return jax.vmap(lambda level_id, node_id: node_gens(gen_key, level_id, node_id))(level_ids.reshape(-1), node_ids.reshape(-1))


def draw_chain_gens(key, part):
    device = jnp.arange(DEVICES, dtype=jnp.int32)[:, None]
    depths = jnp.arange(1, IN_LEVELS + 1, dtype=jnp.int32)[None, :]
    level_ids = jnp.broadcast_to(LOCAL_LEVELS + depths, (DEVICES, IN_LEVELS))
    node_ids = jnp.right_shift(device, depths)
    gen_key = jax.random.fold_in(key, 13)
    return jax.vmap(lambda level_id, node_id: node_gens(gen_key, level_id, node_id))(level_ids.reshape(-1), node_ids.reshape(-1))


def draw_node_ranks(key, part):
    ranks = jax.random.randint(jax.random.fold_in(key, 14), (LEVELS, LEAVES), 3 * RANK // 4, RANK + 1, jnp.int32)
    return ranks.at[0, 0].set(RANK).at[0, 1].set(3 * RANK // 4)


def setup_inputs(seed: int = 0) -> dict:
    keys = jax.random.split(jax.random.key(seed), 6)
    return {
        "leaf_blocks": draw_leaf_blocks(jax.random.fold_in(keys[5], 71), 0),
        "leaf_bases": draw_leaf_bases(jax.random.fold_in(keys[5], 71), 0),
        "local_gens": draw_local_gens(jax.random.fold_in(keys[5], 71), 0),
        "chain_gens": draw_chain_gens(jax.random.fold_in(keys[5], 71), 0),
        "node_ranks": draw_node_ranks(jax.random.fold_in(keys[5], 71), 0),
    }


PRECISE = lax.Precision.HIGHEST

def column_mask(ranks, rank_width):
    return (jnp.arange(rank_width, dtype=jnp.int32)[None, :] < ranks[:, None]).astype(jnp.float32)

def reduce_node(node_block, node_basis, col_mask):
    factor = jnp.linalg.cholesky(node_block)
    whitened = lax.linalg.triangular_solve(factor, node_basis, left_side=True, lower=True)
    gram_matrix = jnp.dot(whitened.T, whitened, precision=PRECISE) + jnp.diag(1.0 - col_mask)
    gram_factor = jnp.linalg.cholesky(gram_matrix)
    identity = jnp.eye(col_mask.shape[0], dtype=jnp.float32)
    inverse_factor = lax.linalg.triangular_solve(gram_factor, identity, left_side=True, lower=True)
    reduced = jnp.dot(inverse_factor.T, inverse_factor, precision=PRECISE)
    return reduced * col_mask[:, None] * col_mask[None, :]

def assemble(reduced_left, reduced_right, couple_left, couple_right, mask_left, mask_right):
    coupling = (couple_left + couple_right.T) * mask_left[:, None] * mask_right[None, :]
    upper_half = jnp.concatenate([reduced_left, coupling], axis=1)
    lower_half = jnp.concatenate([coupling.T, reduced_right], axis=1)
    row_mask = jnp.concatenate([mask_left, mask_right])
    node_block = jnp.concatenate([upper_half, lower_half], axis=0) + jnp.diag(1.0 - row_mask)
    return (node_block, row_mask)

def merge_pair(reduced_left, reduced_right, gens_left, gens_right, mask_left, mask_right, mask_parent):
    node_block, row_mask = assemble(reduced_left, reduced_right, gens_left[1], gens_right[1], mask_left, mask_right)
    node_basis = jnp.concatenate([gens_left[0], gens_right[0]], axis=0) * row_mask[:, None] * mask_parent[None, :]
    return reduce_node(node_block, node_basis, mask_parent)

def reference(leaf_blocks, leaf_bases, local_gens, chain_gens, node_ranks):
    rank_width = RANK
    local_all = local_gens.reshape(DEVICES, 2 * LEAF_DEV - 1, 2, rank_width, rank_width)
    chain_all = chain_gens.reshape(DEVICES, IN_LEVELS, 2, rank_width, rank_width)
    col_mask = column_mask(node_ranks[0], rank_width)
    reduced = lax.map(lambda element: reduce_node(element[0], element[1] * element[2][None, :], element[2]), (leaf_blocks, leaf_bases, col_mask))
    local_parts = [reduced.reshape(DEVICES, LEAF_DEV, rank_width, rank_width)]
    chain_parts = []
    offset = 0
    top_blocks = None
    for tree_level in range(LOCAL_LEVELS + IN_LEVELS + 1):
        node_count = LEAVES >> tree_level
        if tree_level <= LOCAL_LEVELS:
            per_device = LEAF_DEV >> tree_level
            generators = local_all[:, offset:offset + per_device].reshape(node_count, 2, rank_width, rank_width)
            offset = offset + per_device
        else:
            group_depth = tree_level - LOCAL_LEVELS
            generators = chain_all[::2 ** group_depth, group_depth - 1]
        col_mask = column_mask(node_ranks[tree_level, :node_count], rank_width)
        pair_args = (reduced[0::2], reduced[1::2], generators[0::2], generators[1::2], col_mask[0::2], col_mask[1::2])
        if tree_level == LOCAL_LEVELS + IN_LEVELS:
            top_blocks = lax.map(lambda element: jnp.linalg.cholesky(assemble(element[0], element[1], element[2][1], element[3][1], element[4], element[5])[0]), pair_args)
        else:
            parent_mask = column_mask(node_ranks[tree_level + 1, :node_count // 2], rank_width)
            reduced = lax.map(lambda element: merge_pair(*element), pair_args + (parent_mask,))
            if tree_level + 1 <= LOCAL_LEVELS:
                local_parts.append(reduced.reshape(DEVICES, LEAF_DEV >> tree_level + 1, rank_width, rank_width))
            else:
                chain_parts.append(jnp.repeat(reduced, 2 ** (tree_level + 1 - LOCAL_LEVELS), axis=0))
    local_reduced = jnp.concatenate(local_parts, axis=1).reshape(DEVICES * (2 * LEAF_DEV - 1), rank_width, rank_width)
    chain_reduced = jnp.stack(chain_parts, axis=1).reshape(DEVICES * IN_LEVELS, rank_width, rank_width)
    top_factor = jnp.repeat(top_blocks, 2 ** (IN_LEVELS + 1), axis=0).reshape(DEVICES * 2 * rank_width, 2 * rank_width)
    return (local_reduced, chain_reduced, top_factor)
```

```python
import functools

import jax
import jax.numpy as jnp
from jax import lax
from jax.experimental import pallas as pl
from jax.experimental.pallas import tpu as pltpu
from jax.sharding import PartitionSpec as P

BLOCK = 32
LANES = 128
SUB = 8


def spread_row(tile, row):
    return jnp.broadcast_to(tile[row : row + 1, :], (SUB, LANES))


def split(x):
    high = x.astype(jnp.bfloat16)
    return high, (x - high.astype(jnp.float32)).astype(jnp.bfloat16)


def mm(a, b, dims):
    return lax.dot_general(a, b, (dims, ((), ())), preferred_element_type=jnp.float32)


def mm3(a, b, dims):
    ah, al = a
    bh, bl = b
    return mm(ah, bh, dims) + (mm(ah, bl, dims) + mm(al, bh, dims))


def eliminate(a_ref, size, keep):
    width = a_ref.shape[1]
    sub_ids = lax.broadcasted_iota(jnp.int32, (SUB, LANES), 0)
    groups = BLOCK // SUB
    for start in range(0, size, BLOCK):
        first = start // LANES
        tiles = [t for t in range(first, width // LANES) if keep.live(start, t)]
        rows = {
            (h, t): a_ref[start + SUB * h : start + SUB * (h + 1), LANES * t : LANES * (t + 1)]
            for h in range(groups)
            for t in tiles
        }
        lane = start % LANES
        cols = [
            {
                h: jnp.broadcast_to(rows[h, first][:, lane + k : lane + k + 1], (SUB, LANES))
                for h in range(k // SUB, groups)
            }
            for k in range(BLOCK)
        ]
        pivots = [None] * groups
        for k in range(BLOCK):
            g, s = divmod(k, SUB)
            pivot = spread_row(cols[k][g], s)
            pivots[g] = pivot if s == 0 else jnp.where(sub_ids >= s, pivot, pivots[g])
            inverse = 1.0 / pivot
            scaled = {h: cols[k][h] * inverse for h in range(g, groups)}
            for m in range(k + 1, BLOCK):
                entry = spread_row(cols[k][m // SUB], m % SUB)
                for h in range(m // SUB, groups):
                    cols[m][h] = cols[m][h] - scaled[h] * entry
            if s < SUB - 1:
                scaled[g] = jnp.where(sub_ids > s, scaled[g], 0.0)
            else:
                del scaled[g]
            for t in tiles:
                source = spread_row(rows[g, t], s)
                for h in scaled:
                    rows[h, t] = rows[h, t] - scaled[h] * source
        roots = [lax.rsqrt(p) for p in pivots]
        lefts, rights = {}, {}
        for t in tiles:
            r = jnp.concatenate([rows[h, t] * roots[h] for h in range(groups)], axis=0)
            high, low = split(r)
            keep(start, t, r, high, low)
            rights[t] = jnp.concatenate([high, low, high, low], axis=0)
            if t < size // LANES:
                hf = high.astype(jnp.float32)
                lf = low.astype(jnp.float32)
                lefts[t] = jnp.concatenate([hf, hf, lf, lf], axis=0).T.astype(jnp.bfloat16)
        after = start + BLOCK
        spans = []
        if after < size:
            spans.append((after, after + BLOCK))
            stop = after + BLOCK
            while stop < size:
                end = min(size, (stop // LANES + 1) * LANES)
                spans.append((stop, end))
                stop = end
        for low_row, high_row in spans:
            rt = low_row // LANES
            used = [t for t in tiles if t >= rt]
            left = lefts[rt][low_row - rt * LANES : high_row - rt * LANES]
            right = jnp.concatenate([rights[t] for t in used], axis=1)
            change = mm(left, right, ((1,), (0,)))
            for i, t in enumerate(used):
                at = (slice(low_row, high_row), slice(LANES * t, LANES * (t + 1)))
                a_ref[at] = a_ref[at] - change[:, LANES * i : LANES * (i + 1)]


class Keep:
    def __init__(self, size, high_ref, low_ref, triangular):
        self.size, self.high_ref, self.low_ref, self.triangular = size, high_ref, low_ref, triangular

    def live(self, start, tile):
        z = tile - self.size // LANES
        return z < 0 or not self.triangular or z <= start // LANES

    def __call__(self, start, tile, r, high, low):
        z = tile - self.size // LANES
        if z >= 0:
            at = (slice(start, start + BLOCK), slice(LANES * z, LANES * (z + 1)))
            self.high_ref[at] = high
            self.low_ref[at] = low


class KeepRows:
    def __init__(self, ref):
        self.ref = ref

    def live(self, start, tile):
        return True

    def __call__(self, start, tile, r, high, low):
        self.ref[start : start + BLOCK, LANES * tile : LANES * (tile + 1)] = r


def gram(high_ref, low_ref):
    pair = (high_ref[...], low_ref[...])
    return mm3(pair, pair, ((0,), (0,)))


def masks(rank, n):
    rows = lax.broadcasted_iota(jnp.int32, (n, n), 0)
    lanes = lax.broadcasted_iota(jnp.int32, (n, n), 1)
    return rows < rank, lanes < rank, ((rows == lanes) & (rows >= rank)).astype(jnp.float32)


def leaf_kernel(info_ref, block_ref, basis_ref, out_ref, a_ref, high_ref, low_ref):
    size, width = basis_ref.shape[1:]
    rank = info_ref[0]
    lanes = lax.broadcasted_iota(jnp.int32, (size, width), 1)
    a_ref[:, :size] = block_ref[0]
    a_ref[:, size:] = jnp.where(lanes < rank, basis_ref[0], 0.0)
    eliminate(a_ref, size, Keep(size, high_ref, low_ref, False))
    out_ref[...] = gram(high_ref, low_ref) + masks(rank, width)[2]


def inverse_kernel(level, info_ref, g_ref, out_ref, a_ref, high_ref, low_ref):
    n = g_ref.shape[0]
    in_rows, in_lanes, _ = masks(info_ref[2 * level], n)
    rows = lax.broadcasted_iota(jnp.int32, (n, n), 0)
    lanes = lax.broadcasted_iota(jnp.int32, (n, n), 1)
    a_ref[:, :n] = g_ref[...]
    a_ref[:, n:] = (rows == lanes).astype(jnp.float32)
    high_ref[...] = jnp.zeros_like(high_ref)
    low_ref[...] = jnp.zeros_like(low_ref)
    eliminate(a_ref, n, Keep(n, high_ref, low_ref, True))
    out_ref[...] = jnp.where(in_rows & in_lanes, gram(high_ref, low_ref), 0.0)


def merge_kernel(
    level, info_ref, reduced_ref, other_g_ref, gens_ref, other_gens_ref, out_ref, a_ref, high_ref, low_ref
):
    n = reduced_ref.shape[0]
    own_rows, own_lanes, own_rest = masks(info_ref[2 * level], n)
    other_rows, _, _ = masks(info_ref[2 * level + 1], n)
    _, parent_lanes, parent_rest = masks(info_ref[2 * level + 2], n)
    coupling = jnp.where(other_rows & own_lanes, other_gens_ref[1] + gens_ref[0, 1].T, 0.0)
    other_basis = jnp.where(other_rows & parent_lanes, other_gens_ref[0], 0.0)
    left = split(jnp.concatenate([coupling, other_basis], axis=1))
    solved = mm3(split(other_g_ref[...]), left, ((1,), (0,)))
    product = mm3(left, split(solved), ((0,), (0,)))
    a_ref[:, :n] = reduced_ref[...] + own_rest - product[:n, :n]
    a_ref[:, n:] = jnp.where(own_rows & parent_lanes, gens_ref[0, 0], 0.0) - product[:n, n:]
    eliminate(a_ref, n, Keep(n, high_ref, low_ref, False))
    out_ref[...] = product[n:, n:] + parent_rest + gram(high_ref, low_ref)


def top_kernel(
    level, info_ref, reduced_ref, g_ref, other_g_ref, gens_ref, other_couple_ref, out_ref, cross_ref, a_ref, r_ref
):
    n = reduced_ref.shape[0]
    is_left = info_ref[2 * level + 2] == 1
    own_rows, own_lanes, own_rest = masks(info_ref[2 * level], n)
    other_rows, other_lanes, _ = masks(info_ref[2 * level + 1], n)
    own_couple, other_couple = gens_ref[0, 0], other_couple_ref[...]
    couple_left = jnp.where(is_left, own_couple, other_couple)
    couple_right = jnp.where(is_left, other_couple, own_couple)
    left_rank = jnp.where(is_left, info_ref[2 * level], info_ref[2 * level + 1])
    right_rank = jnp.where(is_left, info_ref[2 * level + 1], info_ref[2 * level])
    rows = lax.broadcasted_iota(jnp.int32, (n, n), 0)
    lanes = lax.broadcasted_iota(jnp.int32, (n, n), 1)
    coupling = jnp.where((rows < right_rank) & (lanes < left_rank), couple_right + couple_left.T, 0.0)
    g_left = jnp.where(is_left, g_ref[...], other_g_ref[...])
    coupling = split(coupling)
    cross = mm3(coupling, split(g_left), ((1,), (0,)))
    cross_ref[...] = cross
    change = mm3(split(cross), coupling, ((1,), (1,)))
    a_ref[...] = reduced_ref[...] + own_rest - jnp.where(is_left, 0.0, change)
    eliminate(a_ref, n, KeepRows(r_ref))
    for i in range(0, n, LANES):
        for j in range(0, n, LANES):
            at = (slice(i, i + LANES), slice(j, j + LANES))
            if j > i:
                out_ref[at] = jnp.zeros((LANES, LANES), jnp.float32)
            else:
                tile = r_ref[j : j + LANES, i : i + LANES].T
                if i == j:
                    keep = lax.broadcasted_iota(jnp.int32, tile.shape, 0) >= lax.broadcasted_iota(
                        jnp.int32, tile.shape, 1
                    )
                    tile = jnp.where(keep, tile, 0.0)
                out_ref[at] = tile


def final_kernel(level, info_ref, own_ref, other_ref, cross_ref, out_ref):
    n = own_ref.shape[0]
    is_left = info_ref[2 * level + 2] == 1
    own, other = own_ref[...], other_ref[...]
    left = jnp.where(is_left, own, other)
    out_ref[:n, :n] = left
    out_ref[:n, n:] = jnp.zeros((n, n), jnp.float32)
    out_ref[n:, :n] = mm3(split(cross_ref[...]), split(left), ((1,), (0,)))
    out_ref[n:, n:] = jnp.where(is_left, other, own)


def call(kernel, name, outs, scratch, operands, specs, flops):
    whole = pl.BlockSpec(memory_space=pltpu.VMEM)
    shapes = [jax.ShapeDtypeStruct(o, jnp.float32) for o in outs]
    moved = sum(4 * x.size for x in operands[1:]) + sum(4 * s.size for s in shapes)
    results = pl.pallas_call(
        kernel,
        grid=(1,),
        in_specs=[pl.BlockSpec(memory_space=pltpu.SMEM)]
        + [s if s is not None else whole for s in specs],
        out_specs=[whole] * len(shapes),
        out_shape=shapes,
        scratch_shapes=scratch,
        compiler_params=pltpu.CompilerParams(vmem_limit_bytes=24 * 2**20),
        cost_estimate=pl.CostEstimate(flops=flops, bytes_accessed=moved, transcendentals=0),
        name=name,
    )(*operands)
    return results if len(outs) > 1 else results[0]


def partner(x, axis, bit):
    return lax.ppermute(x, axis, [(i, i ^ 1 << bit) for i in range(lax.axis_size(axis))])


def body(leaf_blocks, leaf_bases, local_gens, chain_gens, node_ranks):
    size, n = leaf_bases.shape[1:]
    in_levels = chain_gens.shape[0]
    outer_pos = lax.axis_index("outer")
    device = outer_pos * lax.axis_size("inner") + lax.axis_index("inner")

    levels = jnp.arange(in_levels + 1, dtype=jnp.int32)
    own_nodes = jnp.right_shift(device, levels)
    nodes = jnp.stack([own_nodes, jnp.bitwise_xor(own_nodes, 1)], axis=1)
    hit = jnp.arange(node_ranks.shape[1], dtype=jnp.int32)[None, None, :] == nodes[:, :, None]
    ranks = jnp.sum(jnp.where(hit, node_ranks[:, None, :], 0), axis=2).reshape(-1)
    is_left = 1 - jnp.bitwise_and(outer_pos, 1)
    info = jnp.concatenate([ranks, is_left[None]]).astype(jnp.int32)

    other_gens = [partner(local_gens[0], "inner", 0)]
    for depth in range(1, in_levels):
        other_gens.append(partner(chain_gens[depth - 1], "inner", depth))
    other_couple = partner(chain_gens[in_levels - 1, 1], "outer", 0)

    def scratch(rows):
        return [
            pltpu.VMEM((rows, rows + n), jnp.float32),
            pltpu.VMEM((rows, n), jnp.bfloat16),
            pltpu.VMEM((rows, n), jnp.bfloat16),
        ]

    g = call(leaf_kernel, "leaf", [(n, n)], scratch(size), (info, leaf_blocks, leaf_bases), [None] * 2, 15 * 2**30)
    reduced = []
    for level in range(in_levels + 1):
        other_g = partner(g, "inner", level) if level < in_levels else partner(g, "outer", 0)
        inverse = call(
            functools.partial(inverse_kernel, level), f"inverse{level}", [(n, n)], scratch(n), (info, g), [None], 7 * 2**30
        )
        reduced.append(inverse)
        if level < in_levels:
            gens = local_gens if level == 0 else chain_gens
            at = max(level - 1, 0)
            g = call(
                functools.partial(merge_kernel, level),
                f"merge{level}",
                [(n, n)],
                scratch(n),
                (info, inverse, other_g, gens, other_gens[level]),
                [None, None, pl.BlockSpec((1, 2, n, n), lambda i, at=at: (at, 0, 0, 0)), None],
                8 * 2**30,
            )
    factor, cross = call(
        functools.partial(top_kernel, in_levels),
        "top",
        [(n, n), (n, n)],
        [pltpu.VMEM((n, n), jnp.float32)] * 2,
        (info, reduced[-1], g, other_g, chain_gens, other_couple),
        [None, None, None, pl.BlockSpec((1, 1, n, n), lambda i: (in_levels - 1, 1, 0, 0)), None],
        7 * 2**30,
    )
    other_factor = partner(factor, "outer", 0)
    top_factor = call(
        functools.partial(final_kernel, in_levels),
        "final",
        [(2 * n, 2 * n)],
        [],
        (info, factor, other_factor, cross),
        [None] * 3,
        2**28,
    )
    return (reduced[0][None], jnp.stack(reduced[1:], axis=0), top_factor)


def solution(mesh):
    return jax.shard_map(
        body,
        mesh=mesh,
        in_specs=(
            P(("outer", "inner"), None, None),
            P(("outer", "inner"), None, None),
            P(("outer", "inner"), None, None, None),
            P(("outer", "inner"), None, None, None),
            P(),
        ),
        out_specs=(
            P(("outer", "inner"), None, None),
            P(("outer", "inner"), None, None),
            P(("outer", "inner"), None),
        ),
        check_vma=False,
    )
```

```python
import functools

import jax
import jax.numpy as jnp
from jax import lax
from jax.experimental import pallas as pl
from jax.experimental.pallas import tpu as pltpu
from jax.sharding import PartitionSpec as P

BLOCK = 16
REACH = 16
LANES = 128
SUB = 8


def spread_row(tile, row):
    return jnp.broadcast_to(tile[row : row + 1, :], (SUB, LANES))


def split(x):
    high = x.astype(jnp.bfloat16)
    return high, (x - high.astype(jnp.float32)).astype(jnp.bfloat16)


def mm(a, b, dims):
    return lax.dot_general(a, b, (dims, ((), ())), preferred_element_type=jnp.float32)


def mm3(a, b, dims):
    ah, al = a
    bh, bl = b
    return mm(ah, bh, dims) + (mm(ah, bl, dims) + mm(al, bh, dims))


def eliminate(a_ref, size, keep, landed=None):
    width = a_ref.shape[1]
    sub_ids = lax.broadcasted_iota(jnp.int32, (SUB, LANES), 0)
    groups = BLOCK // SUB
    for start in range(0, size, BLOCK):
        first = start // LANES
        tiles = [t for t in range(first, width // LANES) if keep.live(start, t)]
        window = min(start + BLOCK + REACH, size)
        total = (window - start) // SUB
        rows = {
            (h, t): a_ref[start + SUB * h : start + SUB * (h + 1), LANES * t : LANES * (t + 1)]
            for h in range(total)
            for t in tiles
        }
        lane = start % LANES
        cols = [
            {
                h: jnp.broadcast_to(rows[h, first][:, lane + k : lane + k + 1], (SUB, LANES))
                for h in range(k // SUB, total)
            }
            for k in range(BLOCK)
        ]
        pivots = [None] * groups
        for k in range(BLOCK):
            g, s = divmod(k, SUB)
            pivot = spread_row(cols[k][g], s)
            pivots[g] = pivot if s == 0 else jnp.where(sub_ids >= s, pivot, pivots[g])
            inverse = 1.0 / pivot
            scaled = {h: cols[k][h] * inverse for h in range(g, total)}
            for m in range(k + 1, BLOCK):
                entry = spread_row(cols[k][m // SUB], m % SUB)
                for h in range(m // SUB, total):
                    cols[m][h] = cols[m][h] - scaled[h] * entry
            if s < SUB - 1:
                scaled[g] = jnp.where(sub_ids > s, scaled[g], 0.0)
            else:
                del scaled[g]
            for t in tiles:
                source = spread_row(rows[g, t], s)
                for h in scaled:
                    rows[h, t] = rows[h, t] - scaled[h] * source
        for h in range(groups, total):
            for t in tiles:
                a_ref[start + SUB * h : start + SUB * (h + 1), LANES * t : LANES * (t + 1)] = rows[h, t]
        roots = [lax.rsqrt(p) for p in pivots]
        lefts, rights = {}, {}
        for t in tiles:
            r = jnp.concatenate([rows[h, t] * roots[h] for h in range(groups)], axis=0)
            high, low = split(r)
            keep(start, t, r, high, low)
            rights[t] = jnp.concatenate([high, low, high, low], axis=0)
            if t < size // LANES and LANES * (t + 1) > window:
                lefts[t] = jnp.concatenate([high, high, low, low], axis=0).T
        if landed is not None and start == 0:
            landed()
        spans = []
        at = window
        while at < size:
            end = at + BLOCK if at == window else min(size, (at // LANES + 1) * LANES)
            spans.append((at, end))
            at = end
        for low_row, high_row in spans:
            rt = low_row // LANES
            used = [t for t in tiles if t >= rt or low_row % LANES < REACH]
            left = lefts[rt][low_row - rt * LANES : high_row - rt * LANES]
            right = jnp.concatenate([rights[t] for t in used], axis=1)
            change = mm(left, right, ((1,), (0,)))
            for i, t in enumerate(used):
                at = (slice(low_row, high_row), slice(LANES * t, LANES * (t + 1)))
                a_ref[at] = a_ref[at] - change[:, LANES * i : LANES * (i + 1)]


class Keep:
    def __init__(self, size, high_ref, low_ref, triangular):
        self.size, self.high_ref, self.low_ref, self.triangular = size, high_ref, low_ref, triangular

    def live(self, start, tile):
        z = tile - self.size // LANES
        return z < 0 or not self.triangular or z <= start // LANES

    def __call__(self, start, tile, r, high, low):
        z = tile - self.size // LANES
        if z >= 0:
            at = (slice(start, start + BLOCK), slice(LANES * z, LANES * (z + 1)))
            self.high_ref[at] = high
            self.low_ref[at] = low


class KeepRows:
    def __init__(self, ref):
        self.ref = ref

    def live(self, start, tile):
        return True

    def __call__(self, start, tile, r, high, low):
        self.ref[start : start + BLOCK, LANES * tile : LANES * (tile + 1)] = r


def gram(high_ref, low_ref):
    pair = (high_ref[...], low_ref[...])
    return mm3(pair, pair, ((0,), (0,)))


def masks(rank, n):
    rows = lax.broadcasted_iota(jnp.int32, (n, n), 0)
    lanes = lax.broadcasted_iota(jnp.int32, (n, n), 1)
    return rows < rank, lanes < rank, jnp.where((rows == lanes) & (rows >= rank), 1.0, 0.0)


def own_rank(info_ref, level):
    return info_ref[3 * level : 3 * level + 1, :]


def other_rank(info_ref, level):
    return info_ref[3 * level + 1 : 3 * level + 2, :]


def is_left(info_ref, level):
    return info_ref[3 * level + 2 : 3 * level + 3, :] == 0


def leaf_kernel(info_ref, block_ref, basis_ref, out_ref, a_ref, high_ref, low_ref, sems):
    size, width = basis_ref.shape[1:]

    def pieces(low, high, sem):
        return [
            pltpu.make_async_copy(
                block_ref.at[0, low:high, :], a_ref.at[low:high, :size], sems.at[sem]
            ),
            pltpu.make_async_copy(
                basis_ref.at[0, low:high, :], a_ref.at[low:high, size:], sems.at[sem + 1]
            ),
        ]

    now = pieces(0, BLOCK + REACH, 0)
    later = pieces(BLOCK + REACH, size, 2)
    for copy in now + later:
        copy.start()
    for copy in now:
        copy.wait()

    def landed():
        for copy in later:
            copy.wait()

    eliminate(a_ref, size, Keep(size, high_ref, low_ref, False), landed)
    in_rows, in_lanes, rest = masks(own_rank(info_ref, 0), width)
    out_ref[...] = jnp.where(in_rows & in_lanes, gram(high_ref, low_ref), rest)


def inverse_kernel(level, info_ref, g_ref, out_ref, a_ref, high_ref, low_ref):
    n = g_ref.shape[0]
    in_rows, in_lanes, _ = masks(own_rank(info_ref, level), n)
    rows = lax.broadcasted_iota(jnp.int32, (n, n), 0)
    lanes = lax.broadcasted_iota(jnp.int32, (n, n), 1)
    a_ref[:, :n] = g_ref[...]
    a_ref[:, n:] = jnp.where(rows == lanes, 1.0, 0.0)
    high_ref[...] = jnp.zeros_like(high_ref)
    low_ref[...] = jnp.zeros_like(low_ref)
    eliminate(a_ref, n, Keep(n, high_ref, low_ref, True))
    out_ref[...] = jnp.where(in_rows & in_lanes, gram(high_ref, low_ref), 0.0)


def merge_kernel(
    level, row, info_ref, reduced_ref, other_g_ref, gens_ref, other_gens_ref, *refs
):
    out_ref, kept_ref, a_ref, high_ref, low_ref, sem = refs[-6:]
    n = reduced_ref.shape[0]
    save = pltpu.make_async_copy(reduced_ref, kept_ref.at[row], sem)
    save.start()
    own_rows, own_lanes, own_rest = masks(own_rank(info_ref, level), n)
    other_rows, _, _ = masks(other_rank(info_ref, level), n)
    _, parent_lanes, parent_rest = masks(own_rank(info_ref, level + 1), n)
    coupling = jnp.where(other_rows & own_lanes, other_gens_ref[1] + gens_ref[row, 1].T, 0.0)
    other_basis = jnp.where(other_rows & parent_lanes, other_gens_ref[0], 0.0)
    joint = split(jnp.concatenate([coupling, other_basis], axis=1))
    solved = mm3(split(other_g_ref[...]), joint, ((1,), (0,)))
    product = mm3(joint, split(solved), ((0,), (0,)))
    a_ref[:, :n] = reduced_ref[...] + own_rest - product[:n, :n]
    a_ref[:, n:] = jnp.where(own_rows & parent_lanes, gens_ref[row, 0], 0.0) - product[:n, n:]
    eliminate(a_ref, n, Keep(n, high_ref, low_ref, False))
    out_ref[...] = product[n:, n:] + parent_rest + gram(high_ref, low_ref)
    save.wait()


def top_kernel(
    info_ref, reduced_ref, g_ref, other_g_ref, gens_ref, other_couple_ref, kept_in_ref,
    out_ref, cross_ref, kept_ref, a_ref, r_ref, sem,
):
    levels = gens_ref.shape[0]
    n = g_ref.shape[0]
    save = pltpu.make_async_copy(reduced_ref, kept_ref.at[levels - 1], sem)
    save.start()
    left = is_left(info_ref, levels)
    own, other = own_rank(info_ref, levels), other_rank(info_ref, levels)
    own_rest = masks(own, n)[2]
    own_couple, other_couple = gens_ref[levels - 1, 1], other_couple_ref[...]
    couple_left = jnp.where(left, own_couple, other_couple)
    couple_right = jnp.where(left, other_couple, own_couple)
    rows = lax.broadcasted_iota(jnp.int32, (n, n), 0)
    lanes = lax.broadcasted_iota(jnp.int32, (n, n), 1)
    inside = (rows < jnp.where(left, other, own)) & (lanes < jnp.where(left, own, other))
    coupling = split(jnp.where(inside, couple_right + couple_left.T, 0.0))
    cross = mm3(coupling, split(jnp.where(left, g_ref[...], other_g_ref[...])), ((1,), (0,)))
    cross_ref[...] = cross
    change = mm3(split(cross), coupling, ((1,), (1,)))
    a_ref[...] = reduced_ref[...] + own_rest - jnp.where(left, 0.0, change)
    eliminate(a_ref, n, KeepRows(r_ref))
    for i in range(0, n, LANES):
        for j in range(0, n, LANES):
            at = (slice(i, i + LANES), slice(j, j + LANES))
            if j > i:
                out_ref[at] = jnp.zeros((LANES, LANES), jnp.float32)
                continue
            tile = r_ref[j : j + LANES, i : i + LANES].T
            if i == j:
                tile = jnp.where(rows[:LANES, :LANES] >= lanes[:LANES, :LANES], tile, 0.0)
            out_ref[at] = tile
    save.wait()


def final_kernel(level, info_ref, own_ref, other_ref, cross_ref, out_ref, parts_ref, sems):
    n = own_ref.shape[0]
    left = is_left(info_ref, level)
    own, other = own_ref[...], other_ref[...]
    places = [(0, 0), (1, 1), (0, 1), (1, 0)]
    copies = [
        pltpu.make_async_copy(
            parts_ref.at[q], out_ref.at[n * i : n * (i + 1), n * j : n * (j + 1)], sems.at[q]
        )
        for q, (i, j) in enumerate(places)
    ]
    factor = jnp.where(left, own, other)
    parts_ref[0] = factor
    copies[0].start()
    parts_ref[1] = jnp.where(left, other, own)
    copies[1].start()
    parts_ref[2] = jnp.zeros((n, n), jnp.float32)
    copies[2].start()
    parts_ref[3] = mm3(split(cross_ref[...]), split(factor), ((1,), (0,)))
    copies[3].start()
    for copy in copies:
        copy.wait()


def call(kernel, name, outs, scratch, operands, flops, in_hbm=(), out_hbm=(), aliases=None):
    vmem = pl.BlockSpec(memory_space=pltpu.VMEM)
    hbm = pl.BlockSpec(memory_space=pltpu.MemorySpace.HBM)
    shapes = [jax.ShapeDtypeStruct(o, jnp.float32) for o in outs]
    moved = sum(4 * x.size for x in operands) + sum(4 * s.size for s in shapes)
    results = pl.pallas_call(
        kernel,
        in_specs=[hbm if i in in_hbm else vmem for i in range(len(operands))],
        out_specs=[hbm if i in out_hbm else vmem for i in range(len(outs))],
        out_shape=shapes,
        scratch_shapes=scratch,
        input_output_aliases=aliases or {},
        compiler_params=pltpu.CompilerParams(vmem_limit_bytes=24 * 2**20),
        cost_estimate=pl.CostEstimate(flops=flops, bytes_accessed=moved, transcendentals=0),
        name=name,
    )(*operands)
    return results if len(outs) > 1 else results[0]


def partner(x, axis, bit):
    return lax.ppermute(x, axis, [(i, i ^ 1 << bit) for i in range(lax.axis_size(axis))])


def body(leaf_blocks, leaf_bases, local_gens, chain_gens, node_ranks):
    size, n = leaf_bases.shape[1:]
    in_levels = chain_gens.shape[0]
    outer_pos = lax.axis_index("outer")
    device = outer_pos * lax.axis_size("inner") + lax.axis_index("inner")

    other_gens = [partner(local_gens[0], "inner", 0)]
    for depth in range(1, in_levels):
        other_gens.append(partner(chain_gens[depth - 1], "inner", depth))
    other_couple = partner(chain_gens[in_levels - 1, 1], "outer", 0)

    levels = jnp.arange(in_levels + 1, dtype=jnp.int32)
    own_nodes = jnp.right_shift(device, levels)
    nodes = jnp.stack([own_nodes, jnp.bitwise_xor(own_nodes, 1)], axis=1)
    hit = jnp.arange(node_ranks.shape[1], dtype=jnp.int32)[None, None, :] == nodes[:, :, None]
    ranks = jnp.sum(jnp.where(hit, node_ranks[:, None, :], 0), axis=2)
    info = jnp.concatenate([ranks, jnp.bitwise_and(own_nodes, 1)[:, None]], axis=1).reshape(-1)
    info = jnp.broadcast_to(jnp.pad(info, (0, -info.shape[0] % 8))[:, None], (-(-info.shape[0] // 8) * 8, n))

    def scratch(rows):
        return [
            pltpu.VMEM((rows, rows + n), jnp.float32),
            pltpu.VMEM((rows, n), jnp.bfloat16),
            pltpu.VMEM((rows, n), jnp.bfloat16),
        ]

    g = call(
        leaf_kernel,
        "leaf",
        [(n, n)],
        scratch(size) + [pltpu.SemaphoreType.DMA((4,))],
        (info, leaf_blocks, leaf_bases),
        15 * 2**30,
        in_hbm=(1, 2),
    )
    for level in range(in_levels + 1):
        other_g = partner(g, "inner", level) if level < in_levels else partner(g, "outer", 0)
        inverse = call(
            functools.partial(inverse_kernel, level), f"inverse{level}", [(n, n)], scratch(n), (info, g), 2**20
        )
        if level == in_levels:
            break
        gens = chain_gens if level else local_gens
        operands = (info, inverse, other_g, gens, other_gens[level])
        linked = level > 1
        g, kept = call(
            functools.partial(merge_kernel, level, max(level - 1, 0)),
            f"merge{level}",
            [(n, n), (in_levels if level else 1, n, n)],
            scratch(n) + [pltpu.SemaphoreType.DMA(())],
            operands + ((kept,) if linked else ()),
            8 * 2**30,
            in_hbm=(5,),
            out_hbm=(1,),
            aliases={5: 1} if linked else None,
        )
        if level == 0:
            local_reduced = kept
    factor, cross, chain_reduced = call(
        top_kernel,
        "top",
        [(n, n), (n, n), (in_levels, n, n)],
        [pltpu.VMEM((n, n), jnp.float32)] * 2 + [pltpu.SemaphoreType.DMA(())],
        (info, inverse, g, other_g, chain_gens, other_couple, kept),
        7 * 2**30,
        in_hbm=(6,),
        out_hbm=(2,),
        aliases={6: 2},
    )
    other_factor = partner(factor, "outer", 0)
    top_factor = call(
        functools.partial(final_kernel, in_levels),
        "final",
        [(2 * n, 2 * n)],
        [pltpu.VMEM((4, n, n), jnp.float32), pltpu.SemaphoreType.DMA((4,))],
        (info, factor, other_factor, cross),
        2**28,
        out_hbm=(0,),
    )
    return (local_reduced, chain_reduced, top_factor)


def solution(mesh):
    return jax.shard_map(
        body,
        mesh=mesh,
        in_specs=(
            P(("outer", "inner"), None, None),
            P(("outer", "inner"), None, None),
            P(("outer", "inner"), None, None, None),
            P(("outer", "inner"), None, None, None),
            P(),
        ),
        out_specs=(
            P(("outer", "inner"), None, None),
            P(("outer", "inner"), None, None),
            P(("outer", "inner"), None),
        ),
        check_vma=False,
    )
```

```python
import functools

import jax
import jax.numpy as jnp
from jax import lax
from jax.experimental import pallas as pl
from jax.experimental.pallas import tpu as pltpu
from jax.sharding import PartitionSpec as P

BLOCK = 16
REACH = 16
LANES = 128
SUB = 8


def spread_row(tile, row):
    return jnp.broadcast_to(tile[row : row + 1, :], (SUB, LANES))


def split(x):
    high = x.astype(jnp.bfloat16)
    return high, (x - high.astype(jnp.float32)).astype(jnp.bfloat16)


def mm(a, b, dims):
    return lax.dot_general(a, b, (dims, ((), ())), preferred_element_type=jnp.float32)


def mm3(a, b, dims):
    ah, al = a
    bh, bl = b
    return mm(ah, bh, dims) + (mm(ah, bl, dims) + mm(al, bh, dims))


def eliminate(a_ref, size, keep, landed=None):
    width = a_ref.shape[1]
    sub_ids = lax.broadcasted_iota(jnp.int32, (SUB, LANES), 0)
    groups = BLOCK // SUB
    for start in range(0, size, BLOCK):
        first = start // LANES
        tiles = [t for t in range(first, width // LANES) if keep.live(start, t)]
        window = min(start + BLOCK + REACH, size)
        total = (window - start) // SUB
        rows = {
            (h, t): a_ref[start + SUB * h : start + SUB * (h + 1), LANES * t : LANES * (t + 1)]
            for h in range(total)
            for t in tiles
        }
        lane = start % LANES
        cols = [
            {
                h: jnp.broadcast_to(rows[h, first][:, lane + k : lane + k + 1], (SUB, LANES))
                for h in range(k // SUB, total)
            }
            for k in range(BLOCK)
        ]
        pivots = [None] * groups
        for k in range(BLOCK):
            g, s = divmod(k, SUB)
            pivot = spread_row(cols[k][g], s)
            pivots[g] = pivot if s == 0 else jnp.where(sub_ids >= s, pivot, pivots[g])
            inverse = 1.0 / pivot
            scaled = {h: cols[k][h] * inverse for h in range(g, total)}
            for m in range(k + 1, BLOCK):
                entry = spread_row(cols[k][m // SUB], m % SUB)
                for h in range(m // SUB, total):
                    cols[m][h] = cols[m][h] - scaled[h] * entry
            if s < SUB - 1:
                scaled[g] = jnp.where(sub_ids > s, scaled[g], 0.0)
            else:
                del scaled[g]
            for t in tiles:
                source = spread_row(rows[g, t], s)
                for h in scaled:
                    rows[h, t] = rows[h, t] - scaled[h] * source
        for h in range(groups, total):
            for t in tiles:
                a_ref[start + SUB * h : start + SUB * (h + 1), LANES * t : LANES * (t + 1)] = rows[h, t]
        roots = [lax.rsqrt(p) for p in pivots]
        lefts, rights = {}, {}
        for t in tiles:
            r = jnp.concatenate([rows[h, t] * roots[h] for h in range(groups)], axis=0)
            high, low = split(r)
            keep(start, t, r, high, low)
            rights[t] = jnp.concatenate([high, low, high, low], axis=0)
            if t < size // LANES and LANES * (t + 1) > window:
                lefts[t] = jnp.concatenate([high, high, low, low], axis=0).T
        if landed is not None and start == 0:
            landed()
        spans = []
        at = window
        while at < size:
            end = at + BLOCK if at == window else min(size, (at // LANES + 1) * LANES)
            spans.append((at, end))
            at = end
        for low_row, high_row in spans:
            rt = low_row // LANES
            used = [t for t in tiles if t >= rt or low_row % LANES < REACH]
            left = lefts[rt][low_row - rt * LANES : high_row - rt * LANES]
            right = jnp.concatenate([rights[t] for t in used], axis=1)
            change = mm(left, right, ((1,), (0,)))
            for i, t in enumerate(used):
                at = (slice(low_row, high_row), slice(LANES * t, LANES * (t + 1)))
                a_ref[at] = a_ref[at] - change[:, LANES * i : LANES * (i + 1)]


class Keep:
    def __init__(self, size, high_ref, low_ref, triangular):
        self.size, self.high_ref, self.low_ref, self.triangular = size, high_ref, low_ref, triangular

    def live(self, start, tile):
        z = tile - self.size // LANES
        return z < 0 or not self.triangular or z <= start // LANES

    def __call__(self, start, tile, r, high, low):
        z = tile - self.size // LANES
        if z >= 0:
            at = (slice(start, start + BLOCK), slice(LANES * z, LANES * (z + 1)))
            self.high_ref[at] = high
            self.low_ref[at] = low


class KeepRows:
    def __init__(self, ref):
        self.ref = ref

    def live(self, start, tile):
        return True

    def __call__(self, start, tile, r, high, low):
        self.ref[start : start + BLOCK, LANES * tile : LANES * (tile + 1)] = r


def gram(high_ref, low_ref):
    pair = (high_ref[...], low_ref[...])
    return mm3(pair, pair, ((0,), (0,)))


def masks(rank, n):
    rows = lax.broadcasted_iota(jnp.int32, (n, n), 0)
    lanes = lax.broadcasted_iota(jnp.int32, (n, n), 1)
    return rows < rank, lanes < rank, jnp.where((rows == lanes) & (rows >= rank), 1.0, 0.0)


def own_rank(info_ref, level):
    return info_ref[3 * level : 3 * level + 1, :]


def other_rank(info_ref, level):
    return info_ref[3 * level + 1 : 3 * level + 2, :]


def is_left(info_ref, level):
    return info_ref[3 * level + 2 : 3 * level + 3, :] == 0


def fill_info(device_ref, ranks_ref, info_ref):
    levels, nodes = ranks_ref.shape
    lanes = lax.broadcasted_iota(jnp.int32, (1, nodes), 1)
    device = device_ref[...]
    width = info_ref.shape[1]
    for level in range(levels):
        node = jnp.right_shift(device, level)
        ranks = ranks_ref[level : level + 1, :].astype(jnp.float32)
        for i, wanted in enumerate((node, jnp.bitwise_xor(node, 1))):
            rank = jnp.sum(jnp.where(lanes == wanted, ranks, 0.0), axis=1, keepdims=True)
            info_ref[3 * level + i : 3 * level + i + 1, :] = jnp.broadcast_to(rank, (1, width)).astype(jnp.int32)
        side = jnp.bitwise_and(node[:, :1], 1)
        info_ref[3 * level + 2 : 3 * level + 3, :] = jnp.broadcast_to(side, (1, width))


def leaf_kernel(device_ref, ranks_ref, block_ref, basis_ref, chain_ref, out_ref, info_ref, *refs):
    a_ref, high_ref, low_ref, sems = refs[-4:]
    size, width = basis_ref.shape[1:]
    slices = [
        pltpu.make_async_copy(chain_ref.at[i], ref, sems.at[4 + i]) for i, ref in enumerate(refs[:-4])
    ]

    def pieces(low, high, sem):
        return [
            pltpu.make_async_copy(
                block_ref.at[0, low:high, :], a_ref.at[low:high, :size], sems.at[sem]
            ),
            pltpu.make_async_copy(
                basis_ref.at[0, low:high, :], a_ref.at[low:high, size:], sems.at[sem + 1]
            ),
        ]

    now = pieces(0, BLOCK + REACH, 0)
    later = pieces(BLOCK + REACH, size, 2)
    for copy in now + later + slices:
        copy.start()
    fill_info(device_ref, ranks_ref, info_ref)
    for copy in now:
        copy.wait()

    def landed():
        for copy in later:
            copy.wait()

    eliminate(a_ref, size, Keep(size, high_ref, low_ref, False), landed)
    in_rows, in_lanes, rest = masks(own_rank(info_ref, 0), width)
    out_ref[0] = jnp.where(in_rows & in_lanes, gram(high_ref, low_ref), rest)
    for copy in slices:
        copy.wait()


def inverse_kernel(level, info_ref, g_ref, out_ref, a_ref, high_ref, low_ref):
    n = g_ref.shape[1]
    in_rows, in_lanes, _ = masks(own_rank(info_ref, level), n)
    rows = lax.broadcasted_iota(jnp.int32, (n, n), 0)
    lanes = lax.broadcasted_iota(jnp.int32, (n, n), 1)
    a_ref[:, :n] = g_ref[0]
    a_ref[:, n:] = jnp.where(rows == lanes, 1.0, 0.0)
    high_ref[...] = jnp.zeros_like(high_ref)
    low_ref[...] = jnp.zeros_like(low_ref)
    eliminate(a_ref, n, Keep(n, high_ref, low_ref, True))
    out_ref[...] = jnp.where(in_rows & in_lanes, gram(high_ref, low_ref), 0.0)


def merge_kernel(
    level, row, info_ref, reduced_ref, other_g_ref, gens_ref, other_gens_ref, *refs
):
    out_ref, kept_ref, a_ref, high_ref, low_ref, sem = refs[-6:]
    n = reduced_ref.shape[0]
    save = pltpu.make_async_copy(reduced_ref, kept_ref.at[row], sem)
    save.start()
    own_rows, own_lanes, own_rest = masks(own_rank(info_ref, level), n)
    other_rows, _, _ = masks(other_rank(info_ref, level), n)
    _, parent_lanes, parent_rest = masks(own_rank(info_ref, level + 1), n)
    coupling = jnp.where(other_rows & own_lanes, other_gens_ref[1] + gens_ref[row, 1].T, 0.0)
    other_basis = jnp.where(other_rows & parent_lanes, other_gens_ref[0], 0.0)
    coupling, other_basis = split(coupling), split(other_basis)
    joint = [jnp.concatenate(pair, axis=1) for pair in zip(coupling, other_basis)]
    solved = split(mm3(split(other_g_ref[0]), joint, ((1,), (0,))))
    product = mm3(coupling, solved, ((0,), (0,)))
    a_ref[:, :n] = reduced_ref[...] + own_rest - product[:n, :n]
    a_ref[:, n:] = jnp.where(own_rows & parent_lanes, gens_ref[row, 0], 0.0) - product[:n, n:]

    def landed():
        out_ref[0] = parent_rest + mm3(other_basis, [half[:, n:] for half in solved], ((0,), (0,)))
        if out_ref.shape[0] > 1:
            out_ref[1] = gens_ref[gens_ref.shape[0] - 1, 1]

    eliminate(a_ref, n, Keep(n, high_ref, low_ref, False), landed)
    out_ref[0] = out_ref[0] + gram(high_ref, low_ref)
    save.wait()


def top_kernel(
    info_ref, reduced_ref, g_ref, other_g_ref, kept_in_ref,
    out_ref, cross_ref, kept_ref, a_ref, r_ref, sem,
):
    levels = kept_ref.shape[0]
    n = reduced_ref.shape[0]
    save = pltpu.make_async_copy(reduced_ref, kept_ref.at[levels - 1], sem)
    save.start()
    left = is_left(info_ref, levels)
    own, other = own_rank(info_ref, levels), other_rank(info_ref, levels)
    own_rest = masks(own, n)[2]
    own_couple, other_couple = g_ref[1], other_g_ref[1]
    couple_left = jnp.where(left, own_couple, other_couple)
    couple_right = jnp.where(left, other_couple, own_couple)
    rows = lax.broadcasted_iota(jnp.int32, (n, n), 0)
    lanes = lax.broadcasted_iota(jnp.int32, (n, n), 1)
    inside = (rows < jnp.where(left, other, own)) & (lanes < jnp.where(left, own, other))
    coupling = split(jnp.where(inside, couple_right + couple_left.T, 0.0))
    cross = mm3(coupling, split(jnp.where(left, g_ref[0], other_g_ref[0])), ((1,), (0,)))
    cross_ref[...] = cross
    change = mm3(split(cross), coupling, ((1,), (1,)))
    a_ref[...] = reduced_ref[...] + own_rest - jnp.where(left, 0.0, change)
    eliminate(a_ref, n, KeepRows(r_ref))
    for i in range(0, n, LANES):
        for j in range(0, n, LANES):
            at = (slice(i, i + LANES), slice(j, j + LANES))
            if j > i:
                out_ref[at] = jnp.zeros((LANES, LANES), jnp.float32)
                continue
            tile = r_ref[j : j + LANES, i : i + LANES].T
            if i == j:
                tile = jnp.where(rows[:LANES, :LANES] >= lanes[:LANES, :LANES], tile, 0.0)
            out_ref[at] = tile
    save.wait()


def final_kernel(level, info_ref, own_ref, other_ref, cross_ref, out_ref, parts_ref, sems):
    n = own_ref.shape[0]
    left = is_left(info_ref, level)
    own, other = own_ref[...], other_ref[...]
    places = [(0, 0), (1, 1), (0, 1), (1, 0)]
    copies = [
        pltpu.make_async_copy(
            parts_ref.at[q], out_ref.at[n * i : n * (i + 1), n * j : n * (j + 1)], sems.at[q]
        )
        for q, (i, j) in enumerate(places)
    ]
    factor = jnp.where(left, own, other)
    parts_ref[0] = factor
    copies[0].start()
    parts_ref[1] = jnp.where(left, other, own)
    copies[1].start()
    parts_ref[2] = jnp.zeros((n, n), jnp.float32)
    copies[2].start()
    parts_ref[3] = mm3(split(cross_ref[...]), split(factor), ((1,), (0,)))
    copies[3].start()
    for copy in copies:
        copy.wait()


def call(kernel, name, outs, scratch, operands, flops, in_hbm=(), out_hbm=(), aliases=None, types=None, vmem_mib=24):
    vmem = pl.BlockSpec(memory_space=pltpu.VMEM)
    hbm = pl.BlockSpec(memory_space=pltpu.MemorySpace.HBM)
    types = types or [jnp.float32] * len(outs)
    shapes = [jax.ShapeDtypeStruct(o, t) for o, t in zip(outs, types)]
    moved = sum(4 * x.size for x in operands) + sum(4 * s.size for s in shapes)
    results = pl.pallas_call(
        kernel,
        in_specs=[hbm if i in in_hbm else vmem for i in range(len(operands))],
        out_specs=[hbm if i in out_hbm else vmem for i in range(len(outs))],
        out_shape=shapes,
        scratch_shapes=scratch,
        input_output_aliases=aliases or {},
        compiler_params=pltpu.CompilerParams(vmem_limit_bytes=vmem_mib * 2**20),
        cost_estimate=pl.CostEstimate(flops=flops, bytes_accessed=moved, transcendentals=0),
        name=name,
    )(*operands)
    return results if len(outs) > 1 else results[0]


def partner(x, axis, bit):
    return lax.ppermute(x, axis, [(i, i ^ 1 << bit) for i in range(lax.axis_size(axis))])


def body(leaf_blocks, leaf_bases, local_gens, chain_gens, node_ranks):
    size, n = leaf_bases.shape[1:]
    in_levels = chain_gens.shape[0]
    outer_pos = lax.axis_index("outer")
    device = outer_pos * lax.axis_size("inner") + lax.axis_index("inner")

    def scratch(rows):
        return [
            pltpu.VMEM((rows, rows + n), jnp.float32),
            pltpu.VMEM((rows, n), jnp.bfloat16),
            pltpu.VMEM((rows, n), jnp.bfloat16),
        ]

    other_gens = [partner(local_gens[0], "inner", 0)]
    levels, nodes = node_ranks.shape
    g, info, *slices = call(
        leaf_kernel,
        "leaf",
        [(1, n, n), (-(-3 * levels // 8) * 8, n)] + [(2, n, n)] * (in_levels - 1),
        scratch(size) + [pltpu.SemaphoreType.DMA((4 + in_levels - 1,))],
        (jnp.full((1, nodes), device, jnp.int32), node_ranks, leaf_blocks, leaf_bases, chain_gens),
        15 * 2**30,
        in_hbm=(2, 3, 4),
        out_hbm=range(2, 1 + in_levels),
        types=[jnp.float32, jnp.int32] + [jnp.float32] * (in_levels - 1),
        vmem_mib=60,
    )
    for depth in range(1, in_levels):
        other_gens.append(partner(slices[depth - 1], "inner", depth))
    for level in range(in_levels + 1):
        other_g = partner(g, "inner", level) if level < in_levels else partner(g, "outer", 0)
        inverse = call(
            functools.partial(inverse_kernel, level), f"inverse{level}", [(n, n)], scratch(n), (info, g), 2**20
        )
        if level == in_levels:
            break
        gens = chain_gens if level else local_gens
        operands = (info, inverse, other_g, gens, other_gens[level])
        linked = level > 1
        g, kept = call(
            functools.partial(merge_kernel, level, max(level - 1, 0)),
            f"merge{level}",
            [(2 if level == in_levels - 1 else 1, n, n), (in_levels if level else 1, n, n)],
            scratch(n) + [pltpu.SemaphoreType.DMA(())],
            operands + ((kept,) if linked else ()),
            8 * 2**30,
            in_hbm=(5,),
            out_hbm=(1,),
            aliases={5: 1} if linked else None,
        )
        if level == 0:
            local_reduced = kept
    factor, cross, chain_reduced = call(
        top_kernel,
        "top",
        [(n, n), (n, n), (in_levels, n, n)],
        [pltpu.VMEM((n, n), jnp.float32)] * 2 + [pltpu.SemaphoreType.DMA(())],
        (info, inverse, g, other_g, kept),
        7 * 2**30,
        in_hbm=(4,),
        out_hbm=(2,),
        aliases={4: 2},
    )
    other_factor = partner(factor, "outer", 0)
    top_factor = call(
        functools.partial(final_kernel, in_levels),
        "final",
        [(2 * n, 2 * n)],
        [pltpu.VMEM((4, n, n), jnp.float32), pltpu.SemaphoreType.DMA((4,))],
        (info, factor, other_factor, cross),
        2**28,
        out_hbm=(0,),
    )
    return (local_reduced, chain_reduced, top_factor)


def solution(mesh):
    return jax.shard_map(
        body,
        mesh=mesh,
        in_specs=(
            P(("outer", "inner"), None, None),
            P(("outer", "inner"), None, None),
            P(("outer", "inner"), None, None, None),
            P(("outer", "inner"), None, None, None),
            P(),
        ),
        out_specs=(
            P(("outer", "inner"), None, None),
            P(("outer", "inner"), None, None),
            P(("outer", "inner"), None),
        ),
        check_vma=False,
    )
```

```python
import functools

import jax
import jax.numpy as jnp
from jax import lax
from jax.experimental import pallas as pl
from jax.experimental.pallas import tpu as pltpu
from jax.sharding import PartitionSpec as P

BLOCK = 16
REACH = 16
LANES = 128
SUB = 8


def spread_row(tile, row):
    return jnp.broadcast_to(tile[row : row + 1, :], (SUB, LANES))


def split(x):
    high = x.astype(jnp.bfloat16)
    return high, (x - high.astype(jnp.float32)).astype(jnp.bfloat16)


def mm(a, b, dims):
    return lax.dot_general(a, b, (dims, ((), ())), preferred_element_type=jnp.float32)


def mm3(a, b, dims):
    ah, al = a
    bh, bl = b
    return mm(ah, bh, dims) + (mm(ah, bl, dims) + mm(al, bh, dims))


def eliminate(a_ref, size, keep, landed=None):
    width = a_ref.shape[1]
    sub_ids = lax.broadcasted_iota(jnp.int32, (SUB, LANES), 0)
    groups = BLOCK // SUB
    for start in range(0, size, BLOCK):
        first = start // LANES
        tiles = [t for t in range(first, width // LANES) if keep.live(start, t)]
        window = min(start + BLOCK + REACH, size)
        total = (window - start) // SUB
        rows = {
            (h, t): a_ref[start + SUB * h : start + SUB * (h + 1), LANES * t : LANES * (t + 1)]
            for h in range(total)
            for t in tiles
        }
        lane = start % LANES
        cols = [
            {
                h: jnp.broadcast_to(rows[h, first][:, lane + k : lane + k + 1], (SUB, LANES))
                for h in range(k // SUB, total)
            }
            for k in range(BLOCK)
        ]
        pivots = [None] * groups
        for k in range(BLOCK):
            g, s = divmod(k, SUB)
            pivot = spread_row(cols[k][g], s)
            pivots[g] = pivot if s == 0 else jnp.where(sub_ids >= s, pivot, pivots[g])
            inverse = 1.0 / pivot
            scaled = {h: cols[k][h] * inverse for h in range(g, total)}
            for m in range(k + 1, BLOCK):
                entry = spread_row(cols[k][m // SUB], m % SUB)
                for h in range(m // SUB, total):
                    cols[m][h] = cols[m][h] - scaled[h] * entry
            if s < SUB - 1:
                scaled[g] = jnp.where(sub_ids > s, scaled[g], 0.0)
            else:
                del scaled[g]
            for t in tiles:
                source = spread_row(rows[g, t], s)
                for h in scaled:
                    rows[h, t] = rows[h, t] - scaled[h] * source
        for h in range(groups, total):
            for t in tiles:
                a_ref[start + SUB * h : start + SUB * (h + 1), LANES * t : LANES * (t + 1)] = rows[h, t]
        roots = [lax.rsqrt(p) for p in pivots]
        lefts, rights = {}, {}
        for t in tiles:
            r = jnp.concatenate([rows[h, t] * roots[h] for h in range(groups)], axis=0)
            high, low = split(r)
            keep(start, t, r, high, low)
            rights[t] = jnp.concatenate([high, low, high, low], axis=0)
            if t < size // LANES and LANES * (t + 1) > window:
                lefts[t] = jnp.concatenate([high, high, low, low], axis=0).T
        if landed is not None and start == 0:
            landed()
        spans = []
        at = window
        while at < size:
            end = at + BLOCK if at == window else min(size, (at // LANES + 1) * LANES)
            spans.append((at, end))
            at = end
        for low_row, high_row in spans:
            rt = low_row // LANES
            used = [t for t in tiles if t >= rt or low_row % LANES < REACH]
            left = lefts[rt][low_row - rt * LANES : high_row - rt * LANES]
            right = jnp.concatenate([rights[t] for t in used], axis=1)
            change = mm(left, right, ((1,), (0,)))
            for i, t in enumerate(used):
                at = (slice(low_row, high_row), slice(LANES * t, LANES * (t + 1)))
                a_ref[at] = a_ref[at] - change[:, LANES * i : LANES * (i + 1)]


class Keep:
    def __init__(self, size, high_ref, low_ref, triangular):
        self.size, self.high_ref, self.low_ref, self.triangular = size, high_ref, low_ref, triangular

    def live(self, start, tile):
        z = tile - self.size // LANES
        return z < 0 or not self.triangular or z <= start // LANES

    def __call__(self, start, tile, r, high, low):
        z = tile - self.size // LANES
        if z >= 0:
            at = (slice(start, start + BLOCK), slice(LANES * z, LANES * (z + 1)))
            self.high_ref[at] = high
            self.low_ref[at] = low


class KeepRows:
    def __init__(self, ref):
        self.ref = ref

    def live(self, start, tile):
        return True

    def __call__(self, start, tile, r, high, low):
        self.ref[start : start + BLOCK, LANES * tile : LANES * (tile + 1)] = r


def gram(high_ref, low_ref):
    pair = (high_ref[...], low_ref[...])
    return mm3(pair, pair, ((0,), (0,)))


def masks(rank, n):
    rows = lax.broadcasted_iota(jnp.int32, (n, n), 0)
    lanes = lax.broadcasted_iota(jnp.int32, (n, n), 1)
    return rows < rank, lanes < rank, jnp.where((rows == lanes) & (rows >= rank), 1.0, 0.0)


def own_rank(info_ref, level):
    return info_ref[3 * level : 3 * level + 1, :]


def other_rank(info_ref, level):
    return info_ref[3 * level + 1 : 3 * level + 2, :]


def is_left(info_ref, level):
    return info_ref[3 * level + 2 : 3 * level + 3, :] == 0


def fill_info(device_ref, ranks_ref, info_ref):
    levels, nodes = ranks_ref.shape
    lanes = lax.broadcasted_iota(jnp.int32, (1, nodes), 1)
    device = device_ref[...]
    width = info_ref.shape[1]
    for level in range(levels):
        node = jnp.right_shift(device, level)
        ranks = ranks_ref[level : level + 1, :].astype(jnp.float32)
        for i, wanted in enumerate((node, jnp.bitwise_xor(node, 1))):
            rank = jnp.sum(jnp.where(lanes == wanted, ranks, 0.0), axis=1, keepdims=True)
            info_ref[3 * level + i : 3 * level + i + 1, :] = jnp.broadcast_to(rank, (1, width)).astype(jnp.int32)
        side = jnp.bitwise_and(node[:, :1], 1)
        info_ref[3 * level + 2 : 3 * level + 3, :] = jnp.broadcast_to(side, (1, width))


def leaf_kernel(device_ref, ranks_ref, block_ref, basis_ref, out_ref, info_ref, a_ref, high_ref, low_ref, sems):
    size, width = basis_ref.shape[1:]

    def pieces(low, high, sem):
        return [
            pltpu.make_async_copy(
                block_ref.at[0, low:high, :], a_ref.at[low:high, :size], sems.at[sem]
            ),
            pltpu.make_async_copy(
                basis_ref.at[0, low:high, :], a_ref.at[low:high, size:], sems.at[sem + 1]
            ),
        ]

    now = pieces(0, BLOCK + REACH, 0)
    later = pieces(BLOCK + REACH, size, 2)
    for copy in now + later:
        copy.start()
    fill_info(device_ref, ranks_ref, info_ref)
    for copy in now:
        copy.wait()

    def landed():
        for copy in later:
            copy.wait()

    eliminate(a_ref, size, Keep(size, high_ref, low_ref, False), landed)
    in_rows, in_lanes, rest = masks(own_rank(info_ref, 0), width)
    out_ref[0] = jnp.where(in_rows & in_lanes, gram(high_ref, low_ref), rest)


def inverse_kernel(level, info_ref, g_ref, out_ref, a_ref, high_ref, low_ref):
    n = g_ref.shape[1]
    in_rows, in_lanes, _ = masks(own_rank(info_ref, level), n)
    rows = lax.broadcasted_iota(jnp.int32, (n, n), 0)
    lanes = lax.broadcasted_iota(jnp.int32, (n, n), 1)
    a_ref[:, :n] = g_ref[0]
    a_ref[:, n:] = jnp.where(rows == lanes, 1.0, 0.0)
    high_ref[...] = jnp.zeros_like(high_ref)
    low_ref[...] = jnp.zeros_like(low_ref)
    eliminate(a_ref, n, Keep(n, high_ref, low_ref, True))
    out_ref[...] = jnp.where(in_rows & in_lanes, gram(high_ref, low_ref), 0.0)


def merge_kernel(
    level, row, info_ref, reduced_ref, other_g_ref, gens_ref, other_gens_ref, *refs
):
    out_ref, kept_ref, a_ref, high_ref, low_ref, sem = refs[-6:]
    n = reduced_ref.shape[0]
    save = pltpu.make_async_copy(reduced_ref, kept_ref.at[row], sem)
    save.start()
    own_rows, own_lanes, own_rest = masks(own_rank(info_ref, level), n)
    other_rows, _, _ = masks(other_rank(info_ref, level), n)
    _, parent_lanes, parent_rest = masks(own_rank(info_ref, level + 1), n)
    coupling = jnp.where(other_rows & own_lanes, other_gens_ref[1] + gens_ref[row, 1].T, 0.0)
    other_basis = jnp.where(other_rows & parent_lanes, other_gens_ref[0], 0.0)
    coupling, other_basis = split(coupling), split(other_basis)
    joint = [jnp.concatenate(pair, axis=1) for pair in zip(coupling, other_basis)]
    solved = split(mm3(split(other_g_ref[0]), joint, ((1,), (0,))))
    product = mm3(coupling, solved, ((0,), (0,)))
    a_ref[:, :n] = reduced_ref[...] + own_rest - product[:n, :n]
    a_ref[:, n:] = jnp.where(own_rows & parent_lanes, gens_ref[row, 0], 0.0) - product[:n, n:]

    def landed():
        out_ref[0] = parent_rest + mm3(other_basis, [half[:, n:] for half in solved], ((0,), (0,)))
        if out_ref.shape[0] > 1:
            out_ref[1] = gens_ref[gens_ref.shape[0] - 1, 1]

    eliminate(a_ref, n, Keep(n, high_ref, low_ref, False), landed)
    out_ref[0] = out_ref[0] + gram(high_ref, low_ref)
    save.wait()


def top_kernel(
    info_ref, reduced_ref, g_ref, other_g_ref, kept_in_ref,
    out_ref, cross_ref, kept_ref, a_ref, r_ref, sem,
):
    levels = kept_ref.shape[0]
    n = reduced_ref.shape[0]
    save = pltpu.make_async_copy(reduced_ref, kept_ref.at[levels - 1], sem)
    save.start()
    left = is_left(info_ref, levels)
    own, other = own_rank(info_ref, levels), other_rank(info_ref, levels)
    own_rest = masks(own, n)[2]
    own_couple, other_couple = g_ref[1], other_g_ref[1]
    couple_left = jnp.where(left, own_couple, other_couple)
    couple_right = jnp.where(left, other_couple, own_couple)
    rows = lax.broadcasted_iota(jnp.int32, (n, n), 0)
    lanes = lax.broadcasted_iota(jnp.int32, (n, n), 1)
    inside = (rows < jnp.where(left, other, own)) & (lanes < jnp.where(left, own, other))
    coupling = split(jnp.where(inside, couple_right + couple_left.T, 0.0))
    cross = mm3(coupling, split(jnp.where(left, g_ref[0], other_g_ref[0])), ((1,), (0,)))
    cross_ref[...] = cross
    change = mm3(split(cross), coupling, ((1,), (1,)))
    a_ref[...] = reduced_ref[...] + own_rest - jnp.where(left, 0.0, change)
    eliminate(a_ref, n, KeepRows(r_ref))
    for i in range(0, n, LANES):
        for j in range(0, n, LANES):
            at = (slice(i, i + LANES), slice(j, j + LANES))
            if j > i:
                out_ref[at] = jnp.zeros((LANES, LANES), jnp.float32)
                continue
            tile = r_ref[j : j + LANES, i : i + LANES].T
            if i == j:
                tile = jnp.where(rows[:LANES, :LANES] >= lanes[:LANES, :LANES], tile, 0.0)
            out_ref[at] = tile
    save.wait()


def final_kernel(level, info_ref, own_ref, other_ref, cross_ref, out_ref, parts_ref, sems):
    n = own_ref.shape[0]
    left = is_left(info_ref, level)
    own, other = own_ref[...], other_ref[...]
    places = [(0, 0), (1, 1), (0, 1), (1, 0)]
    copies = [
        pltpu.make_async_copy(
            parts_ref.at[q], out_ref.at[n * i : n * (i + 1), n * j : n * (j + 1)], sems.at[q]
        )
        for q, (i, j) in enumerate(places)
    ]
    factor = jnp.where(left, own, other)
    parts_ref[0] = factor
    copies[0].start()
    parts_ref[1] = jnp.where(left, other, own)
    copies[1].start()
    parts_ref[2] = jnp.zeros((n, n), jnp.float32)
    copies[2].start()
    parts_ref[3] = mm3(split(cross_ref[...]), split(factor), ((1,), (0,)))
    copies[3].start()
    for copy in copies:
        copy.wait()


def call(kernel, name, outs, scratch, operands, flops, in_hbm=(), out_hbm=(), aliases=None, types=None):
    vmem = pl.BlockSpec(memory_space=pltpu.VMEM)
    hbm = pl.BlockSpec(memory_space=pltpu.MemorySpace.HBM)
    types = types or [jnp.float32] * len(outs)
    shapes = [jax.ShapeDtypeStruct(o, t) for o, t in zip(outs, types)]
    moved = sum(4 * x.size for x in operands) + sum(4 * s.size for s in shapes)
    results = pl.pallas_call(
        kernel,
        in_specs=[hbm if i in in_hbm else vmem for i in range(len(operands))],
        out_specs=[hbm if i in out_hbm else vmem for i in range(len(outs))],
        out_shape=shapes,
        scratch_shapes=scratch,
        input_output_aliases=aliases or {},
        compiler_params=pltpu.CompilerParams(vmem_limit_bytes=24 * 2**20),
        cost_estimate=pl.CostEstimate(flops=flops, bytes_accessed=moved, transcendentals=0),
        name=name,
    )(*operands)
    return results if len(outs) > 1 else results[0]


def partner(x, axis, bit):
    return lax.ppermute(x, axis, [(i, i ^ 1 << bit) for i in range(lax.axis_size(axis))])


def body(leaf_blocks, leaf_bases, local_gens, chain_gens, node_ranks):
    size, n = leaf_bases.shape[1:]
    in_levels = chain_gens.shape[0]
    outer_pos = lax.axis_index("outer")
    device = outer_pos * lax.axis_size("inner") + lax.axis_index("inner")

    def scratch(rows):
        return [
            pltpu.VMEM((rows, rows + n), jnp.float32),
            pltpu.VMEM((rows, n), jnp.bfloat16),
            pltpu.VMEM((rows, n), jnp.bfloat16),
        ]

    other_gens = [partner(local_gens[0], "inner", 0)]
    levels, nodes = node_ranks.shape
    g, info = call(
        leaf_kernel,
        "leaf",
        [(1, n, n), (-(-3 * levels // 8) * 8, n)],
        scratch(size) + [pltpu.SemaphoreType.DMA((4,))],
        (jnp.full((1, nodes), device, jnp.int32), node_ranks, leaf_blocks, leaf_bases),
        15 * 2**30,
        in_hbm=(2, 3),
        types=[jnp.float32, jnp.int32],
    )
    for depth in range(1, in_levels):
        other_gens.append(partner(chain_gens[depth - 1], "inner", depth))
    for level in range(in_levels + 1):
        other_g = partner(g, "inner", level) if level < in_levels else partner(g, "outer", 0)
        inverse = call(
            functools.partial(inverse_kernel, level), f"inverse{level}", [(n, n)], scratch(n), (info, g), 2**20
        )
        if level == in_levels:
            break
        gens = chain_gens if level else local_gens
        operands = (info, inverse, other_g, gens, other_gens[level])
        linked = level > 1
        g, kept = call(
            functools.partial(merge_kernel, level, max(level - 1, 0)),
            f"merge{level}",
            [(2 if level == in_levels - 1 else 1, n, n), (in_levels if level else 1, n, n)],
            scratch(n) + [pltpu.SemaphoreType.DMA(())],
            operands + ((kept,) if linked else ()),
            8 * 2**30,
            in_hbm=(5,),
            out_hbm=(1,),
            aliases={5: 1} if linked else None,
        )
        if level == 0:
            local_reduced = kept
    factor, cross, chain_reduced = call(
        top_kernel,
        "top",
        [(n, n), (n, n), (in_levels, n, n)],
        [pltpu.VMEM((n, n), jnp.float32)] * 2 + [pltpu.SemaphoreType.DMA(())],
        (info, inverse, g, other_g, kept),
        7 * 2**30,
        in_hbm=(4,),
        out_hbm=(2,),
        aliases={4: 2},
    )
    other_factor = partner(factor, "outer", 0)
    top_factor = call(
        functools.partial(final_kernel, in_levels),
        "final",
        [(2 * n, 2 * n)],
        [pltpu.VMEM((4, n, n), jnp.float32), pltpu.SemaphoreType.DMA((4,))],
        (info, factor, other_factor, cross),
        2**28,
        out_hbm=(0,),
    )
    return (local_reduced, chain_reduced, top_factor)


def solution(mesh):
    return jax.shard_map(
        body,
        mesh=mesh,
        in_specs=(
            P(("outer", "inner"), None, None),
            P(("outer", "inner"), None, None),
            P(("outer", "inner"), None, None, None),
            P(("outer", "inner"), None, None, None),
            P(),
        ),
        out_specs=(
            P(("outer", "inner"), None, None),
            P(("outer", "inner"), None, None),
            P(("outer", "inner"), None),
        ),
        check_vma=False,
    )
```
